512 devices in a mesh: gz: 64 (over z, x_lo, core), step: 8 (over y, x_hi).
Axes of the slice: x: 4 (x_hi: 2, x_lo: 2; x = x_hi * 2 + x_lo), y: 4, z: 16, core: 2. Of those that a mesh axis runs over, the one named last changes fastest.
Arguments:
- reference_volume: bfloat16 [512, 16, 32, 128], P('gz', None, 'step'), may hold values from -6 to 6
- deformed: bfloat16 [8, 512, 16, 32, 128], P('step', 'gz'), may hold values from -6 to 6
- centres: int32 [8, 64, 2], P('step', 'gz'), may hold values from 0 to 124
- tether: float32 [64, 2], P('gz'), may hold values from 0.2 to 200
Outputs:
- displacement: float32 [8, 64, 2, 3], P('step', 'gz')
The draws below stay inside these ranges and needn't reach their ends.
All inputs are finite; a program needn't handle non-finite values.
Results may differ from the reference program's by a relative error of at most 0.0003.
Values may be sent and summed in bfloat16 or wider, within the bound.
No kernel may reach another device: no remote copies, remote signals or barrier semaphores. Data moves between devices by JAX's collectives and lax.ppermute only.
A program may use at most 128 MiB of HBM per device.

```python
import math
import jax
import jax.numpy as jnp
from jax import lax

C = 16
PZ = 8
SB = 16
XW = 128
NBY = 2
YW = 32
NZB = 64
NZ = 512
STEPS = 8


def place_ends(values, own_key, smallest, high):
    longest = values.shape.index(max(values.shape))
    spots = []
    for shift in (0, 1):
        where = [jax.random.randint(jax.random.fold_in(own_key, axis), (), 0, length) for axis, length in enumerate(values.shape)]
        where[longest] = (where[longest] + shift) % values.shape[longest]
        spots.append(tuple(where))
    return values.at[spots[0]].set(smallest).at[spots[1]].set(high)


def block_scale(rng, dims, cuts, least, high):
    factor_of, own = 1.0, jax.random.fold_in(rng, 6)
    for position, shards_of in cuts:
        heights = jnp.exp(jax.random.uniform(jax.random.fold_in(own, position), (shards_of,), jnp.float32, least / len(cuts), high / len(cuts)))
        factor_of = factor_of * jnp.repeat(heights, dims[position] // shards_of).reshape([-1 if axis == position else 1 for axis in range(len(dims))])
    return factor_of


def scatter_about(own_key, dims, scale, most, split=(), kind=jnp.bfloat16):
    factor_of = block_scale(own_key, dims, split, -0.22, 0.18) if split else 1.0
    result = jax.random.normal(own_key, dims, jnp.float32) * scale * factor_of
    return jnp.minimum(jnp.maximum(result, -most), most).astype(kind)


def setup_inputs(seed: int = 0) -> dict:
    seeds = jax.random.split(jax.random.key(seed), 5)
    return {
        "reference_volume": scatter_about(seeds[0], (NZ, C, YW, XW), 1.0, 6.0, ((0, 64), (2, 8))),
        "deformed": scatter_about(seeds[1], (STEPS, NZ, C, YW, XW), 1.0, 6.0, ((0, 8), (1, 64))),
        "centres": place_ends(jax.random.randint(seeds[2], (STEPS, NZB, NBY), 0, 125), jax.random.fold_in(seeds[2], 1), 0, 124).astype(jnp.int32),
        "tether": jnp.clip(jnp.exp(math.log(200.0) - 6.9077553 * jax.random.uniform(seeds[3], (NZB, NBY), jnp.float32) ** block_scale(seeds[3], (NZB, NBY), ((0, 64),), -0.2, 0.2)), 0.2, 200.0),
    }


def peak_fit(scores, code_idx, tether):
    cube = scores.reshape(scores.shape[:-1] + (3, 3, 3))
    profiles = [cube.sum(axis=(-2, -1)), cube.sum(axis=(-3, -1)), cube.sum(axis=(-3, -2))]
    offsets = [code_idx // 25 - 2, code_idx // 5 % 5 - 2, code_idx % 5 - 2]
    moves = []
    bends = []
    for profile, offset in zip(profiles, offsets):
        lower = profile[..., 0]
        middle = profile[..., 1]
        upper = profile[..., 2]
        bend = jnp.maximum(2.0 * middle - lower - upper, 1.0)
        delta = jnp.clip((upper - lower) / (2.0 * bend), -1.0, 1.0)
        moves.append(offset.astype(jnp.float32) + delta)
        bends.append(bend)
    measured = jnp.stack(moves, axis=-1)
    quality = (bends[0] + bends[1] + bends[2]) / 3.0
    gain = quality / (quality + tether)
    return (measured, gain)

def reference(reference_volume, deformed, centres, tether):
    norm_factor = 1.0 / math.sqrt(PZ * C * SB * XW)

    def one_step(inputs):
        volume_now, codes = inputs
        padded = jnp.pad(volume_now, ((3, 3), (0, 0), (3, 3), (3, 3)))

        def one_block(index):
            zblock = index // NBY
            yblock = index % NBY
            code_idx = codes[zblock, yblock]
            shift_z = code_idx // 25 - 2
            shift_y = code_idx // 5 % 5 - 2
            shift_x = code_idx % 5 - 2
            window = lax.dynamic_slice(padded, (zblock * PZ + 2 + shift_z, jnp.int32(0), yblock * SB + 2 + shift_y, 2 + shift_x), (PZ + 2, C, SB + 2, XW + 2))
            ref_block = lax.dynamic_slice(reference_volume, (zblock * PZ, jnp.int32(0), yblock * SB, jnp.int32(0)), (PZ, C, SB, XW)).astype(jnp.float32)
            values = []
            for along_z in range(3):
                for along_y in range(3):
                    for along_x in range(3):
                        moved = window[along_z:along_z + PZ, :, along_y:along_y + SB, along_x:along_x + XW].astype(jnp.float32)
                        values.append(jnp.sum(ref_block * moved))
            return jnp.stack(values) * norm_factor
        found = lax.map(one_block, jnp.arange(NZB * NBY, dtype=jnp.int32))
        return found.reshape(NZB, NBY, 27)
    scores = lax.map(one_step, (deformed, centres))
    measured, gain = peak_fit(scores, centres, tether[None])
    zpad = jnp.pad(measured, ((0, 0), (1, 1), (0, 0), (0, 0)))
    zsum = zpad[:, :-2] + 2.0 * zpad[:, 1:-1] + zpad[:, 2:]
    ypad = jnp.pad(zsum, ((0, 0), (0, 0), (1, 1), (0, 0)))
    ysum = ypad[:, :, :-2] + 2.0 * ypad[:, :, 1:-1] + ypad[:, :, 2:]
    zindex = jnp.arange(NZB, dtype=jnp.int32)
    yindex = jnp.arange(NBY, dtype=jnp.int32)
    weight_z = 2.0 + (zindex > 0).astype(jnp.float32) + (zindex < NZB - 1).astype(jnp.float32)
    weight_y = 2.0 + (yindex > 0).astype(jnp.float32) + (yindex < NBY - 1).astype(jnp.float32)
    smooth = ysum / (weight_z[:, None] * weight_y[None, :])[None, :, :, None]
    keep = 1.0 - gain
    drive = gain[..., None] * smooth

    def advance(state, inputs):
        keep_now, drive_now = inputs
        state = keep_now[..., None] * state + drive_now
        return (state, state)
    start_state = jnp.zeros((NZB, NBY, 3), jnp.float32)
    _, tracked = lax.scan(advance, start_state, (keep, drive))
    return tracked
```

```python
import math

import jax
import jax.numpy as jnp
from jax import lax
from jax.experimental import pallas as pl
from jax.experimental.pallas import tpu as pltpu
from jax.sharding import PartitionSpec as P

SB = 16
HALO = 3
PAD = 8


def fit_kernel(
    planes, channels, rows, width,
    code_ref, tether_ref, parity_ref, r_ref, d_ref, inner_ref, outer_ref,
    own_out, edge_out, deep, left, right,
):
    depth = channels * SB
    window = planes + 2
    zeros = jnp.zeros((channels, PAD, width), jnp.float32)
    parity = parity_ref[0]
    inner_at = (1 - parity) * (planes + HALO)
    outer_at = parity * (planes + HALO)
    for z in range(planes + 2 * HALO):
        deep[z, :, 0:PAD, :] = zeros
        deep[z, :, PAD + rows : 2 * PAD + rows, :] = zeros
    for z in range(planes):
        deep[z + HALO, :, PAD : PAD + rows, :] = d_ref[z].astype(jnp.float32)
    for z in range(HALO):
        deep[inner_at + z, :, PAD : PAD + rows, :] = inner_ref[z].astype(jnp.float32)
        deep[outer_at + z, :, PAD : PAD + rows, :] = outer_ref[z].astype(jnp.float32)

    lane = lax.broadcasted_iota(jnp.int32, (1, width), 1)
    line = lax.broadcasted_iota(jnp.int32, (width, width), 0)
    column = lax.broadcasted_iota(jnp.int32, (width, width), 1)
    scale = 1.0 / math.sqrt(planes * depth * width)
    bend_row = jnp.ones((1, width), jnp.float32)
    slope_row = jnp.zeros((1, width), jnp.float32)
    centre_row = jnp.zeros((1, width), jnp.float32)
    quality_row = jnp.ones((1, width), jnp.float32)
    tether_row = jnp.ones((1, width), jnp.float32)
    empty = jnp.zeros((width, depth), jnp.bfloat16)
    for tz in range(3):
        for p in range(window):
            if p < tz or p >= tz + planes:
                left[tz * width : (tz + 1) * width, p * depth : (p + 1) * depth] = empty

    for block in range(rows // SB):
        code = code_ref[0, 0, block]
        shift_z = lax.div(code, 25) - 2
        shift_y = lax.rem(lax.div(code, 5), 5) - 2
        shift_x = lax.rem(code, 5) - 2
        for z in range(planes):
            plane = r_ref[z, :, block * SB : (block + 1) * SB, :].astype(jnp.float32)
            turned = plane.reshape(depth, width).T.astype(jnp.bfloat16)
            for tz in range(3):
                p = z + tz
                left[tz * width : (tz + 1) * width, p * depth : (p + 1) * depth] = turned
        first_plane = shift_z + (HALO - 1)
        first_row = shift_y + (PAD - 1 + block * SB)
        for p in range(window):
            for ty in range(3):
                part = deep[first_plane + p, :, pl.ds(first_row + ty, SB), :]
                right[p * depth : (p + 1) * depth, ty * width : (ty + 1) * width] = (
                    part.reshape(depth, width).astype(jnp.bfloat16)
                )
        gram = jnp.dot(left[...], right[...], preferred_element_type=jnp.float32)
        cut = [
            [
                gram[tz * width : (tz + 1) * width, ty * width : (ty + 1) * width]
                for ty in range(3)
            ]
            for tz in range(3)
        ]
        along_z = [cut[t][0] + cut[t][1] + cut[t][2] for t in range(3)]
        along_y = [cut[0][t] + cut[1][t] + cut[2][t] for t in range(3)]
        whole = along_z[0] + along_z[1] + along_z[2]
        far = column - line - shift_x
        band = jnp.abs(far) <= 1
        upper = jnp.where(far == 1, whole, 0.0)
        lower = jnp.where(far == -1, whole, 0.0)
        middle = jnp.where(far == 0, whole, 0.0)
        bends = [
            jnp.where(band, 2.0 * g[1] - g[0] - g[2], 0.0) for g in (along_z, along_y)
        ] + [2.0 * middle - lower - upper]
        slopes = [jnp.where(band, g[2] - g[0], 0.0) for g in (along_z, along_y)] + [upper - lower]

        def total(values):
            return jnp.sum(jnp.sum(values, axis=0, keepdims=True), axis=1, keepdims=True) * scale

        sums = [jnp.maximum(total(b), 1.0) for b in bends]
        quality = (sums[0] + sums[1] + sums[2]) / 3.0
        for axis, shift in enumerate((shift_z, shift_y, shift_x)):
            here = lane == block * 3 + axis
            bend_row = jnp.where(here, sums[axis], bend_row)
            slope_row = jnp.where(here, total(slopes[axis]), slope_row)
            centre_row = jnp.where(here, shift.astype(jnp.float32), centre_row)
            quality_row = jnp.where(here, quality, quality_row)
            tether_row = jnp.where(here, tether_ref[0, block], tether_row)

    measured = centre_row + jnp.clip(slope_row / (2.0 * bend_row), -1.0, 1.0)
    gain = quality_row / (quality_row + tether_row)
    other = jnp.where(lane < 3, pltpu.roll(measured, width - 3, 1), pltpu.roll(measured, 3, 1))
    used = lane < 6
    filtered = jnp.where(used, 2.0 * measured + other, 0.0)
    gain = jnp.where(used, gain, 0.0)
    own_out[...] = filtered + pltpu.roll(gain, 8, 1)
    edge_out[...] = pltpu.roll(filtered, 16, 1)


def track_kernel(width, place_ref, all_ref, out_ref):
    step = place_ref[0]
    slab = place_ref[1]
    slabs = place_ref[2]
    parity = lax.rem(slab, 2)
    steps = all_ref.shape[0] // 2
    lane = lax.broadcasted_iota(jnp.int32, (1, width), 1)
    weight_z = 2.0 + (slab > 0).astype(jnp.float32) + (slab < slabs - 1).astype(jnp.float32)
    weight = jnp.full((1, width), weight_z * 3.0, jnp.float32)
    state = jnp.zeros((1, width), jnp.float32)
    even = all_ref[0:steps, 0, :]
    odd = all_ref[steps : 2 * steps, 0, :]
    mine = jnp.where(parity == 0, even, odd)
    partner = jnp.where(parity == 0, odd, even)
    gain = pltpu.roll(mine, width - 8, 1)
    outer = pltpu.roll(mine, width - 16, 1)
    smooth = (outer + 2.0 * mine + partner) / weight
    keep = 1.0 - gain
    drive = gain * smooth
    for s in range(steps):
        new = keep[s : s + 1] * state + drive[s : s + 1]
        state = jnp.where(s <= step, new, state)
    state = jnp.where(lane < 6, state, 0.0)
    out_ref[0, 0, 0:1, :] = state[:, 0:3]
    out_ref[0, 0, 1:2, :] = pltpu.roll(state, width - 3, 1)[:, 0:3]


def shards(reference_volume, deformed, centres, tether):
    steps, slabs = lax.axis_size("step"), lax.axis_size("gz")
    slab, step = lax.axis_index("gz"), lax.axis_index("step")
    parity = slab % 2
    volume_now = deformed[0]
    planes, channels, rows, width = volume_now.shape

    copies = jnp.broadcast_to(reference_volume[None], (steps,) + reference_volume.shape)
    gathered = lax.all_to_all(copies, "step", split_axis=0, concat_axis=0, tiled=True)
    whole_ref = gathered.transpose(1, 2, 0, 3, 4).reshape(planes, channels, rows, width)

    inside = [(i, i ^ 1) for i in range(slabs)]
    outside = [(i, i + 1) for i in range(1, slabs - 1, 2)]
    outside = outside + [(j, i) for i, j in outside]
    far = planes - HALO
    to_inner = lax.dynamic_slice_in_dim(volume_now, (1 - parity) * far, HALO, 0)
    to_outer = lax.dynamic_slice_in_dim(volume_now, parity * far, HALO, 0)
    inner = lax.ppermute(to_inner, "gz", inside)
    outer = lax.ppermute(to_outer, "gz", outside)

    smem = pl.BlockSpec(memory_space=pltpu.SMEM)
    vmem = pl.BlockSpec(memory_space=pltpu.VMEM)
    depth = channels * SB
    window = planes + 2
    own, edge = pl.pallas_call(
        lambda *refs: fit_kernel(planes, channels, rows, width, *refs),
        out_shape=[jax.ShapeDtypeStruct((1, width), jnp.float32)] * 2,
        in_specs=[smem] * 3 + [vmem] * 4,
        out_specs=[vmem] * 2,
        scratch_shapes=[
            pltpu.VMEM((planes + 2 * HALO, channels, rows + 2 * PAD, width), jnp.float32),
            pltpu.VMEM((3 * width, window * depth), jnp.bfloat16),
            pltpu.VMEM((window * depth, 3 * width), jnp.bfloat16),
        ],
        compiler_params=pltpu.CompilerParams(vmem_limit_bytes=40 * 1024 * 1024),
        name="fit",
    )(centres, tether, parity[None], whole_ref, volume_now, inner, outer)

    edge = lax.ppermute(edge, "gz", outside)
    row = (own + edge)[None]
    group = 2 * steps
    groups = [[group * i + j for j in range(group)] for i in range(slabs // 2)]
    everyone = lax.all_to_all(
        jnp.broadcast_to(row, (group, 1, width)),
        ("gz", "step"), split_axis=0, concat_axis=0, tiled=True, axis_index_groups=groups,
    )
    place = jnp.stack([step, slab, jnp.int32(slabs)]).astype(jnp.int32)
    return pl.pallas_call(
        lambda *refs: track_kernel(width, *refs),
        out_shape=jax.ShapeDtypeStruct((1, 1, 2, 3), jnp.float32),
        in_specs=[smem, vmem],
        out_specs=vmem,
        name="track",
    )(place, everyone)


def solution(mesh):
    placed = (
        P("gz", None, "step", None),
        P("step", "gz", None, None, None),
        P("step", "gz", None),
        P("gz", None),
    )
    return jax.shard_map(
        shards, mesh=mesh, in_specs=placed, out_specs=P("step", "gz", None, None), check_vma=False
    )
```

```python
import math

import jax
import jax.numpy as jnp
from jax import lax
from jax.experimental import pallas as pl
from jax.experimental.pallas import tpu as pltpu
from jax.sharding import PartitionSpec as P

SB = 16
HALO = 3
PAD = 8
MIB = 1024 * 1024


def offsets(code):
    return (
        lax.div(code, 25) - 2,
        lax.rem(lax.div(code, 5), 5) - 2,
        lax.rem(code, 5) - 2,
    )


def fit_kernel(
    settings_hbm, r_ref, d_ref, inner_ref, outer_ref,
    own_out, edge_out, deep, left, right, settings, arrived
):
    planes, channels, rows, width = r_ref.shape
    depth = channels * SB
    window = planes + 2
    fetch = pltpu.make_async_copy(settings_hbm, settings, arrived)
    fetch.start()
    lane = lax.broadcasted_iota(jnp.int32, (1, width), 1)
    line = lax.broadcasted_iota(jnp.int32, (width, width), 0)
    column = lax.broadcasted_iota(jnp.int32, (width, width), 1)
    scale = 1.0 / math.sqrt(planes * depth * width)
    bend_row = jnp.ones((1, width), jnp.float32)
    slope_row = jnp.zeros((1, width), jnp.float32)
    centre_row = jnp.zeros((1, width), jnp.float32)
    quality_row = jnp.ones((1, width), jnp.float32)
    tether_row = jnp.ones((1, width), jnp.float32)
    empty = jnp.zeros((width, depth), jnp.bfloat16)
    for tz in range(3):
        for p in range(window):
            if p < tz or p >= tz + planes:
                left[tz * width : (tz + 1) * width, p * depth : (p + 1) * depth] = empty
    zeros = jnp.zeros((channels, PAD, width), jnp.float32)
    fetch.wait()
    parity = lax.rem(lax.axis_index("gz"), 2)
    inner_at = (1 - parity) * (planes + HALO)
    outer_at = parity * (planes + HALO)
    for z in range(planes + 2 * HALO):
        deep[z, :, 0:PAD, :] = zeros
        deep[z, :, PAD + rows : 2 * PAD + rows, :] = zeros
    for z in range(HALO):
        deep[inner_at + z, :, PAD : PAD + rows, :] = inner_ref[z].astype(jnp.float32)
        deep[outer_at + z, :, PAD : PAD + rows, :] = outer_ref[z].astype(jnp.float32)
    for z in range(planes):
        deep[z + HALO, :, PAD : PAD + rows, :] = d_ref[z].astype(jnp.float32)

    for block in range(rows // SB):
        shifts = offsets(settings[0, block].astype(jnp.int32))
        for z in range(planes):
            plane = r_ref[z, :, block * SB : (block + 1) * SB, :].astype(jnp.float32)
            turned = plane.reshape(depth, width).T.astype(jnp.bfloat16)
            for tz in range(3):
                p = z + tz
                left[tz * width : (tz + 1) * width, p * depth : (p + 1) * depth] = turned
        first_plane = shifts[0] + (HALO - 1)
        first_row = shifts[1] + (PAD - 1 + block * SB)
        for p in range(window):
            for ty in range(3):
                part = deep[first_plane + p, :, pl.ds(first_row + ty, SB), :]
                right[p * depth : (p + 1) * depth, ty * width : (ty + 1) * width] = (
                    part.reshape(depth, width).astype(jnp.bfloat16)
                )
        gram = jnp.dot(left[...], right[...], preferred_element_type=jnp.float32)
        cut = [
            [
                gram[tz * width : (tz + 1) * width, ty * width : (ty + 1) * width]
                for ty in range(3)
            ]
            for tz in range(3)
        ]
        along_z = [cut[t][0] + cut[t][1] + cut[t][2] for t in range(3)]
        along_y = [cut[0][t] + cut[1][t] + cut[2][t] for t in range(3)]
        whole = along_z[0] + along_z[1] + along_z[2]
        far = column - line - shifts[2]
        band = jnp.abs(far) <= 1
        upper = jnp.where(far == 1, whole, 0.0)
        lower = jnp.where(far == -1, whole, 0.0)
        middle = jnp.where(far == 0, whole, 0.0)
        bends = [
            jnp.where(band, 2.0 * g[1] - g[0] - g[2], 0.0) for g in (along_z, along_y)
        ] + [2.0 * middle - lower - upper]
        slopes = [jnp.where(band, g[2] - g[0], 0.0) for g in (along_z, along_y)] + [upper - lower]

        def total(values):
            return jnp.sum(jnp.sum(values, axis=0, keepdims=True), axis=1, keepdims=True) * scale

        sums = [jnp.maximum(total(b), 1.0) for b in bends]
        quality = (sums[0] + sums[1] + sums[2]) / 3.0
        for axis, shift in enumerate(shifts):
            here = lane == block * 3 + axis
            bend_row = jnp.where(here, sums[axis], bend_row)
            slope_row = jnp.where(here, total(slopes[axis]), slope_row)
            centre_row = jnp.where(here, shift.astype(jnp.float32), centre_row)
            quality_row = jnp.where(here, quality, quality_row)
            tether_row = jnp.where(here, settings[0, rows // SB + block], tether_row)

    measured = centre_row + jnp.clip(slope_row / (2.0 * bend_row), -1.0, 1.0)
    gain = quality_row / (quality_row + tether_row)
    other = jnp.where(lane < 3, pltpu.roll(measured, width - 3, 1), pltpu.roll(measured, 3, 1))
    used = lane < 6
    filtered = jnp.where(used, 2.0 * measured + other, 0.0)
    gain = jnp.where(used, gain, 0.0)
    own_out[...] = filtered + pltpu.roll(gain, 8, 1)
    edge_out[...] = pltpu.roll(filtered, 16, 1)


def track_kernel(all_ref, out_ref):
    step, slab, slabs = lax.axis_index("step"), lax.axis_index("gz"), lax.axis_size("gz")
    parity = lax.rem(slab, 2)
    steps = all_ref.shape[0] // 2
    width = all_ref.shape[2]
    lane = lax.broadcasted_iota(jnp.int32, (1, width), 1)
    weight_z = 2.0 + (slab > 0).astype(jnp.float32) + (slab < slabs - 1).astype(jnp.float32)
    weight = jnp.full((1, width), weight_z * 3.0, jnp.float32)
    state = jnp.zeros((1, width), jnp.float32)
    head = all_ref[0:steps, 0, :]
    tail = all_ref[steps : 2 * steps, 0, :]
    mine = jnp.where(parity == 0, head, tail)
    inner = jnp.where(parity == 0, tail, head)
    outer = pltpu.roll(mine, width - 16, 1)
    gain = pltpu.roll(mine, width - 8, 1)
    smooth = (outer + 2.0 * mine + inner) / weight
    keep = 1.0 - gain
    drive = gain * smooth
    for s in range(steps):
        new = keep[s : s + 1] * state + drive[s : s + 1]
        state = jnp.where(s <= step, new, state)
    state = jnp.where(lane < 6, state, 0.0)
    out_ref[0, 0, 0:1, :] = state[:, 0:3]
    out_ref[0, 0, 1:2, :] = pltpu.roll(state, width - 3, 1)[:, 0:3]


def shards(reference_volume, deformed, centres, tether):
    steps, slabs = lax.axis_size("step"), lax.axis_size("gz")
    slab, step = lax.axis_index("gz"), lax.axis_index("step")
    parity = slab & 1
    volume_now = deformed[0]
    planes, channels, rows, width = volume_now.shape
    depth = channels * SB
    window = planes + 2
    blocks = rows // SB
    vmem = pl.BlockSpec(memory_space=pltpu.VMEM)
    anywhere = pl.BlockSpec(memory_space=pl.ANY)
    like = jax.ShapeDtypeStruct

    inside = [(i, i ^ 1) for i in range(slabs)]
    outside = [(i, i + 1) for i in range(1, slabs - 1, 2)]
    outside = outside + [(j, i) for i, j in outside]
    far = planes - HALO
    to_inner = lax.dynamic_slice_in_dim(volume_now, (1 - parity) * far, HALO, 0)
    to_outer = lax.dynamic_slice_in_dim(volume_now, parity * far, HALO, 0)
    copies = jnp.broadcast_to(reference_volume[None], (steps,) + reference_volume.shape)
    outer = lax.ppermute(to_outer, "gz", outside)
    inner = lax.ppermute(to_inner, "gz", inside)
    gathered = lax.all_to_all(copies, "step", split_axis=0, concat_axis=0, tiled=True)
    whole_ref = gathered.transpose(1, 2, 0, 3, 4).reshape(planes, channels, rows, width)

    settings = jnp.concatenate([centres[0, 0].astype(jnp.float32), tether[0]])[None]
    own, edge = pl.pallas_call(
        fit_kernel,
        out_shape=[like((1, width), jnp.float32)] * 2,
        in_specs=[anywhere] + [vmem] * 4,
        out_specs=[vmem] * 2,
        scratch_shapes=[
            pltpu.VMEM((planes + 2 * HALO, channels, rows + 2 * PAD, width), jnp.float32),
            pltpu.VMEM((3 * width, window * depth), jnp.bfloat16),
            pltpu.VMEM((window * depth, 3 * width), jnp.bfloat16),
            pltpu.SMEM((1, 2 * blocks), jnp.float32),
            pltpu.SemaphoreType.DMA,
        ],
        compiler_params=pltpu.CompilerParams(vmem_limit_bytes=40 * MIB),
        name="fit",
    )(settings, whole_ref, volume_now, inner, outer)

    edge = lax.ppermute(edge, "gz", outside)
    row = (own + edge)[None]
    group = 2 * steps
    groups = [[group * i + j for j in range(group)] for i in range(slabs // 2)]
    everyone = lax.all_to_all(
        jnp.broadcast_to(row, (group, 1, width)),
        ("gz", "step"), split_axis=0, concat_axis=0, tiled=True, axis_index_groups=groups,
    )
    return pl.pallas_call(
        track_kernel,
        out_shape=like((1, 1, blocks, 3), jnp.float32),
        in_specs=[vmem],
        out_specs=vmem,
        compiler_params=pltpu.CompilerParams(vmem_limit_bytes=2 * MIB),
        name="track",
    )(everyone)


def solution(mesh):
    placed = (
        P("gz", None, "step", None),
        P("step", "gz", None, None, None),
        P("step", "gz", None),
        P("gz", None),
    )
    return jax.shard_map(
        shards, mesh=mesh, in_specs=placed, out_specs=P("step", "gz", None, None), check_vma=False
    )
```

```python
import math

import jax
import jax.numpy as jnp
from jax import lax
from jax.experimental import pallas as pl
from jax.experimental.pallas import tpu as pltpu
from jax.sharding import PartitionSpec as P

SB = 16
HALO = 3
PAD = 8
MIB = 1024 * 1024


def offsets(code):
    return (
        lax.div(code, 25) - 2,
        lax.rem(lax.div(code, 5), 5) - 2,
        lax.rem(code, 5) - 2,
    )


def fit_kernel(
    settings_hbm, r_ref, d_ref, inner_ref, outer_ref,
    own_out, edge_out, deep, left_0, left_1, right_0, right_1, settings, arrived
):
    planes, channels, rows, width = r_ref.shape
    depth = channels * SB
    window = planes + 2
    fetch = pltpu.make_async_copy(settings_hbm, settings, arrived)
    fetch.start()
    lane = lax.broadcasted_iota(jnp.int32, (1, width), 1)
    line = lax.broadcasted_iota(jnp.int32, (width, width), 0)
    column = lax.broadcasted_iota(jnp.int32, (width, width), 1)
    scale = 1.0 / math.sqrt(planes * depth * width)
    bend_row = jnp.ones((1, width), jnp.float32)
    slope_row = jnp.zeros((1, width), jnp.float32)
    centre_row = jnp.zeros((1, width), jnp.float32)
    quality_row = jnp.ones((1, width), jnp.float32)
    tether_row = jnp.ones((1, width), jnp.float32)
    empty = jnp.zeros((width, depth), jnp.bfloat16)
    for tz in range(3):
        for p in range(window):
            if p < tz or p >= tz + planes:
                for left in (left_0, left_1):
                    left[tz * width : (tz + 1) * width, p * depth : (p + 1) * depth] = empty
    fetch.wait()
    parity = lax.rem(lax.axis_index("gz"), 2)
    inner_at = (1 - parity) * (planes + HALO)
    outer_at = parity * (planes + HALO)
    for z in range(HALO):
        deep[inner_at + z, :, PAD : PAD + rows, :] = inner_ref[z].astype(jnp.float32)
        deep[outer_at + z, :, PAD : PAD + rows, :] = outer_ref[z].astype(jnp.float32)
    for z in range(planes):
        deep[z + HALO, :, PAD : PAD + rows, :] = d_ref[z].astype(jnp.float32)

    for block in range(rows // SB):
        left, right = ((left_0, right_0), (left_1, right_1))[block]
        shifts = offsets(settings[0, block].astype(jnp.int32))
        for z in range(planes):
            plane = r_ref[z, :, block * SB : (block + 1) * SB, :]
            turned = plane.reshape(depth, width).T
            for tz in range(3):
                p = z + tz
                left[tz * width : (tz + 1) * width, p * depth : (p + 1) * depth] = turned
        first_plane = shifts[0] + (HALO - 1)
        first_row = shifts[1] + (PAD - 1 + block * SB)
        height = lax.broadcasted_iota(jnp.int32, (1, SB, width), 1)
        inside = []
        for ty in range(3):
            row = height + (first_row + ty - PAD)
            inside.append((row >= 0) & (row < rows))
        for p in range(window):
            for ty in range(3):
                part = deep[first_plane + p, :, pl.ds(first_row + ty, SB), :]
                part = jnp.where(inside[ty], part, 0.0)
                right[p * depth : (p + 1) * depth, ty * width : (ty + 1) * width] = (
                    part.reshape(depth, width).astype(jnp.bfloat16)
                )
        gram = jnp.dot(left[...], right[...], preferred_element_type=jnp.float32)
        cut = [
            [
                gram[tz * width : (tz + 1) * width, ty * width : (ty + 1) * width]
                for ty in range(3)
            ]
            for tz in range(3)
        ]
        along_z = [cut[t][0] + cut[t][1] + cut[t][2] for t in range(3)]
        along_y = [cut[0][t] + cut[1][t] + cut[2][t] for t in range(3)]
        whole = along_z[0] + along_z[1] + along_z[2]
        far = column - line - shifts[2]
        band = jnp.abs(far) <= 1
        upper = jnp.where(far == 1, whole, 0.0)
        lower = jnp.where(far == -1, whole, 0.0)
        middle = jnp.where(far == 0, whole, 0.0)
        bends = [
            jnp.where(band, 2.0 * g[1] - g[0] - g[2], 0.0) for g in (along_z, along_y)
        ] + [2.0 * middle - lower - upper]
        slopes = [jnp.where(band, g[2] - g[0], 0.0) for g in (along_z, along_y)] + [upper - lower]

        def total(values):
            return jnp.sum(jnp.sum(values, axis=0, keepdims=True), axis=1, keepdims=True) * scale

        sums = [jnp.maximum(total(b), 1.0) for b in bends]
        quality = (sums[0] + sums[1] + sums[2]) / 3.0
        for axis, shift in enumerate(shifts):
            here = lane == block * 3 + axis
            bend_row = jnp.where(here, sums[axis], bend_row)
            slope_row = jnp.where(here, total(slopes[axis]), slope_row)
            centre_row = jnp.where(here, shift.astype(jnp.float32), centre_row)
            quality_row = jnp.where(here, quality, quality_row)
            tether_row = jnp.where(here, settings[0, rows // SB + block], tether_row)

    measured = centre_row + jnp.clip(slope_row / (2.0 * bend_row), -1.0, 1.0)
    gain = quality_row / (quality_row + tether_row)
    other = jnp.where(lane < 3, pltpu.roll(measured, width - 3, 1), pltpu.roll(measured, 3, 1))
    used = lane < 6
    filtered = jnp.where(used, 2.0 * measured + other, 0.0)
    gain = jnp.where(used, gain, 0.0)
    own_out[...] = filtered + pltpu.roll(gain, 8, 1)
    edge_out[...] = pltpu.roll(filtered, 16, 1)


def track_kernel(all_ref, out_ref):
    step, slab, slabs = lax.axis_index("step"), lax.axis_index("gz"), lax.axis_size("gz")
    parity = lax.rem(slab, 2)
    steps = all_ref.shape[0] // 2
    width = all_ref.shape[2]
    lane = lax.broadcasted_iota(jnp.int32, (1, width), 1)
    weight_z = 2.0 + (slab > 0).astype(jnp.float32) + (slab < slabs - 1).astype(jnp.float32)
    weight = jnp.full((1, width), weight_z * 3.0, jnp.float32)
    state = jnp.zeros((1, width), jnp.float32)
    head = all_ref[0:steps, 0, :]
    tail = all_ref[steps : 2 * steps, 0, :]
    mine = jnp.where(parity == 0, head, tail)
    inner = jnp.where(parity == 0, tail, head)
    outer = pltpu.roll(mine, width - 16, 1)
    gain = pltpu.roll(mine, width - 8, 1)
    smooth = (outer + 2.0 * mine + inner) / weight
    keep = 1.0 - gain
    drive = gain * smooth
    for s in range(steps):
        new = keep[s : s + 1] * state + drive[s : s + 1]
        state = jnp.where(s <= step, new, state)
    state = jnp.where(lane < 6, state, 0.0)
    out_ref[0, 0, 0:1, :] = state[:, 0:3]
    out_ref[0, 0, 1:2, :] = pltpu.roll(state, width - 3, 1)[:, 0:3]


def shards(reference_volume, deformed, centres, tether):
    steps, slabs = lax.axis_size("step"), lax.axis_size("gz")
    slab, step = lax.axis_index("gz"), lax.axis_index("step")
    parity = slab & 1
    volume_now = deformed[0]
    planes, channels, rows, width = volume_now.shape
    depth = channels * SB
    window = planes + 2
    blocks = rows // SB
    vmem = pl.BlockSpec(memory_space=pltpu.VMEM)
    anywhere = pl.BlockSpec(memory_space=pl.ANY)
    like = jax.ShapeDtypeStruct

    inside = [(i, i ^ 1) for i in range(slabs)]
    outside = [(i, i + 1) for i in range(1, slabs - 1, 2)]
    outside = outside + [(j, i) for i, j in outside]
    far = planes - HALO
    to_inner = lax.dynamic_slice_in_dim(volume_now, (1 - parity) * far, HALO, 0)
    to_outer = lax.dynamic_slice_in_dim(volume_now, parity * far, HALO, 0)
    copies = jnp.broadcast_to(reference_volume[None], (steps,) + reference_volume.shape)
    outer = lax.ppermute(to_outer, "gz", outside)
    inner = lax.ppermute(to_inner, "gz", inside)
    gathered = lax.all_to_all(copies, "step", split_axis=0, concat_axis=0, tiled=True)
    whole_ref = gathered.transpose(1, 2, 0, 3, 4).reshape(planes, channels, rows, width)

    settings = jnp.concatenate([centres[0, 0].astype(jnp.float32), tether[0]])[None]
    own, edge = pl.pallas_call(
        fit_kernel,
        out_shape=[like((1, width), jnp.float32)] * 2,
        in_specs=[anywhere] + [vmem] * 4,
        out_specs=[vmem] * 2,
        scratch_shapes=[
            pltpu.VMEM((planes + 2 * HALO, channels, rows + 2 * PAD, width), jnp.float32),
            *([pltpu.VMEM((3 * width, window * depth), jnp.bfloat16)] * blocks),
            *([pltpu.VMEM((window * depth, 3 * width), jnp.bfloat16)] * blocks),
            pltpu.SMEM((1, 2 * blocks), jnp.float32),
            pltpu.SemaphoreType.DMA,
        ],
        compiler_params=pltpu.CompilerParams(vmem_limit_bytes=40 * MIB),
        name="fit",
    )(settings, whole_ref, volume_now, inner, outer)

    edge = lax.ppermute(edge, "gz", outside)
    row = (own + edge)[None]
    group = 2 * steps
    groups = [[group * i + j for j in range(group)] for i in range(slabs // 2)]
    everyone = lax.all_to_all(
        jnp.broadcast_to(row, (group, 1, width)),
        ("gz", "step"), split_axis=0, concat_axis=0, tiled=True, axis_index_groups=groups,
    )
    return pl.pallas_call(
        track_kernel,
        out_shape=like((1, 1, blocks, 3), jnp.float32),
        in_specs=[vmem],
        out_specs=vmem,
        compiler_params=pltpu.CompilerParams(vmem_limit_bytes=2 * MIB),
        name="track",
    )(everyone)


def solution(mesh):
    placed = (
        P("gz", None, "step", None),
        P("step", "gz", None, None, None),
        P("step", "gz", None),
        P("gz", None),
    )
    return jax.shard_map(
        shards, mesh=mesh, in_specs=placed, out_specs=P("step", "gz", None, None), check_vma=False
    )
```

```python
import math

import jax
import jax.numpy as jnp
from jax import lax
from jax.experimental import pallas as pl
from jax.experimental.pallas import tpu as pltpu
from jax.sharding import PartitionSpec as P

SB = 16
HALO = 3
PAD = 8
MIB = 1024 * 1024


def offsets(code):
    return (
        lax.div(code, 25) - 2,
        lax.rem(lax.div(code, 5), 5) - 2,
        lax.rem(code, 5) - 2,
    )


def fit_kernel(
    settings_hbm, r_ref, d_ref, inner_ref, outer_ref,
    own_out, edge_out, deep, left, right, settings, arrived
):
    planes, channels, rows, width = r_ref.shape
    depth = channels * SB
    window = planes + 2
    fetch = pltpu.make_async_copy(settings_hbm, settings, arrived)
    fetch.start()
    lane = lax.broadcasted_iota(jnp.int32, (1, width), 1)
    line = lax.broadcasted_iota(jnp.int32, (width, width), 0)
    column = lax.broadcasted_iota(jnp.int32, (width, width), 1)
    scale = 1.0 / math.sqrt(planes * depth * width)
    bend_row = jnp.ones((1, width), jnp.float32)
    slope_row = jnp.zeros((1, width), jnp.float32)
    centre_row = jnp.zeros((1, width), jnp.float32)
    quality_row = jnp.ones((1, width), jnp.float32)
    tether_row = jnp.ones((1, width), jnp.float32)
    empty = jnp.zeros((width, depth), jnp.bfloat16)
    for tz in range(3):
        for p in range(window):
            if p < tz or p >= tz + planes:
                left[tz * width : (tz + 1) * width, p * depth : (p + 1) * depth] = empty
    zeros = jnp.zeros((channels, PAD, width), jnp.float32)
    fetch.wait()
    parity = lax.rem(lax.axis_index("gz"), 2)
    inner_at = (1 - parity) * (planes + HALO)
    outer_at = parity * (planes + HALO)
    for z in range(planes + 2 * HALO):
        deep[z, :, 0:PAD, :] = zeros
        deep[z, :, PAD + rows : 2 * PAD + rows, :] = zeros
    for z in range(HALO):
        deep[inner_at + z, :, PAD : PAD + rows, :] = inner_ref[z].astype(jnp.float32)
        deep[outer_at + z, :, PAD : PAD + rows, :] = outer_ref[z].astype(jnp.float32)
    for z in range(planes):
        deep[z + HALO, :, PAD : PAD + rows, :] = d_ref[z].astype(jnp.float32)

    for block in range(rows // SB):
        shifts = offsets(settings[0, block].astype(jnp.int32))
        for z in range(planes):
            plane = r_ref[z, :, block * SB : (block + 1) * SB, :].astype(jnp.float32)
            turned = plane.reshape(depth, width).T.astype(jnp.bfloat16)
            for tz in range(3):
                p = z + tz
                left[tz * width : (tz + 1) * width, p * depth : (p + 1) * depth] = turned
        first_plane = shifts[0] + (HALO - 1)
        first_row = shifts[1] + (PAD - 1 + block * SB)
        for p in range(window):
            for ty in range(3):
                part = deep[first_plane + p, :, pl.ds(first_row + ty, SB), :]
                right[p * depth : (p + 1) * depth, ty * width : (ty + 1) * width] = (
                    part.reshape(depth, width).astype(jnp.bfloat16)
                )
        gram = jnp.dot(left[...], right[...], preferred_element_type=jnp.float32)
        cut = [
            [
                gram[tz * width : (tz + 1) * width, ty * width : (ty + 1) * width]
                for ty in range(3)
            ]
            for tz in range(3)
        ]
        along_z = [cut[t][0] + cut[t][1] + cut[t][2] for t in range(3)]
        along_y = [cut[0][t] + cut[1][t] + cut[2][t] for t in range(3)]
        whole = along_z[0] + along_z[1] + along_z[2]
        far = column - line - shifts[2]
        band = jnp.abs(far) <= 1
        upper = jnp.where(far == 1, whole, 0.0)
        lower = jnp.where(far == -1, whole, 0.0)
        middle = jnp.where(far == 0, whole, 0.0)
        bends = [
            jnp.where(band, 2.0 * g[1] - g[0] - g[2], 0.0) for g in (along_z, along_y)
        ] + [2.0 * middle - lower - upper]
        slopes = [jnp.where(band, g[2] - g[0], 0.0) for g in (along_z, along_y)] + [upper - lower]

        def total(values):
            return jnp.sum(jnp.sum(values, axis=0, keepdims=True), axis=1, keepdims=True) * scale

        sums = [jnp.maximum(total(b), 1.0) for b in bends]
        quality = (sums[0] + sums[1] + sums[2]) / 3.0
        for axis, shift in enumerate(shifts):
            here = lane == block * 3 + axis
            bend_row = jnp.where(here, sums[axis], bend_row)
            slope_row = jnp.where(here, total(slopes[axis]), slope_row)
            centre_row = jnp.where(here, shift.astype(jnp.float32), centre_row)
            quality_row = jnp.where(here, quality, quality_row)
            tether_row = jnp.where(here, settings[0, rows // SB + block], tether_row)

    measured = centre_row + jnp.clip(slope_row / (2.0 * bend_row), -1.0, 1.0)
    gain = quality_row / (quality_row + tether_row)
    other = jnp.where(lane < 3, pltpu.roll(measured, width - 3, 1), pltpu.roll(measured, 3, 1))
    used = lane < 6
    filtered = jnp.where(used, 2.0 * measured + other, 0.0)
    gain = jnp.where(used, gain, 0.0)
    own_out[...] = filtered + pltpu.roll(gain, 8, 1)
    edge_out[...] = pltpu.roll(filtered, 16, 1)


def track_kernel(all_ref, out_ref):
    step, slab, slabs = lax.axis_index("step"), lax.axis_index("gz"), lax.axis_size("gz")
    parity = lax.rem(slab, 2)
    steps = all_ref.shape[0] // 2
    width = all_ref.shape[2]
    lane = lax.broadcasted_iota(jnp.int32, (1, width), 1)
    weight_z = 2.0 + (slab > 0).astype(jnp.float32) + (slab < slabs - 1).astype(jnp.float32)
    weight = jnp.full((1, width), weight_z * 3.0, jnp.float32)
    state = jnp.zeros((1, width), jnp.float32)
    head = all_ref[0:steps, 0, :]
    tail = all_ref[steps : 2 * steps, 0, :]
    mine = jnp.where(parity == 0, head, tail)
    inner = jnp.where(parity == 0, tail, head)
    outer = pltpu.roll(mine, width - 16, 1)
    gain = pltpu.roll(mine, width - 8, 1)
    smooth = (outer + 2.0 * mine + inner) / weight
    keep = 1.0 - gain
    drive = gain * smooth
    for s in range(steps):
        new = keep[s : s + 1] * state + drive[s : s + 1]
        state = jnp.where(s <= step, new, state)
    state = jnp.where(lane < 6, state, 0.0)
    out_ref[0, 0, 0:1, :] = state[:, 0:3]
    out_ref[0, 0, 1:2, :] = pltpu.roll(state, width - 3, 1)[:, 0:3]


def shards(reference_volume, deformed, centres, tether):
    steps, slabs = lax.axis_size("step"), lax.axis_size("gz")
    slab, step = lax.axis_index("gz"), lax.axis_index("step")
    parity = slab & 1
    volume_now = deformed[0]
    planes, channels, rows, width = volume_now.shape
    depth = channels * SB
    window = planes + 2
    blocks = rows // SB
    vmem = pl.BlockSpec(memory_space=pltpu.VMEM)
    anywhere = pl.BlockSpec(memory_space=pl.ANY)
    like = jax.ShapeDtypeStruct

    inside = [(i, i ^ 1) for i in range(slabs)]
    outside = [(i, i + 1) for i in range(1, slabs - 1, 2)]
    outside = outside + [(j, i) for i, j in outside]
    far = planes - HALO
    to_inner = lax.dynamic_slice_in_dim(volume_now, (1 - parity) * far, HALO, 0)
    to_outer = lax.dynamic_slice_in_dim(volume_now, parity * far, HALO, 0)
    flat = reference_volume.reshape(-1, width)
    copies = lax.optimization_barrier(jnp.broadcast_to(flat[None], (steps,) + flat.shape))
    copies = copies.reshape((steps,) + reference_volume.shape)
    outer = lax.ppermute(to_outer, "gz", outside)
    inner = lax.ppermute(to_inner, "gz", inside)
    gathered = lax.all_to_all(copies, "step", split_axis=0, concat_axis=0, tiled=True)
    whole_ref = gathered.transpose(1, 2, 0, 3, 4).reshape(planes, channels, rows, width)

    settings = jnp.concatenate([centres[0, 0].astype(jnp.float32), tether[0]])[None]
    own, edge = pl.pallas_call(
        fit_kernel,
        out_shape=[like((1, width), jnp.float32)] * 2,
        in_specs=[anywhere] + [vmem] * 4,
        out_specs=[vmem] * 2,
        scratch_shapes=[
            pltpu.VMEM((planes + 2 * HALO, channels, rows + 2 * PAD, width), jnp.float32),
            pltpu.VMEM((3 * width, window * depth), jnp.bfloat16),
            pltpu.VMEM((window * depth, 3 * width), jnp.bfloat16),
            pltpu.SMEM((1, 2 * blocks), jnp.float32),
            pltpu.SemaphoreType.DMA,
        ],
        compiler_params=pltpu.CompilerParams(vmem_limit_bytes=40 * MIB),
        name="fit",
    )(settings, whole_ref, volume_now, inner, outer)

    edge = lax.ppermute(edge, "gz", outside)
    row = (own + edge)[None]
    group = 2 * steps
    groups = [[group * i + j for j in range(group)] for i in range(slabs // 2)]
    everyone = lax.all_to_all(
        jnp.broadcast_to(row, (group, 1, width)),
        ("gz", "step"), split_axis=0, concat_axis=0, tiled=True, axis_index_groups=groups,
    )
    return pl.pallas_call(
        track_kernel,
        out_shape=like((1, 1, blocks, 3), jnp.float32),
        in_specs=[vmem],
        out_specs=vmem,
        compiler_params=pltpu.CompilerParams(vmem_limit_bytes=2 * MIB),
        name="track",
    )(everyone)


def solution(mesh):
    placed = (
        P("gz", None, "step", None),
        P("step", "gz", None, None, None),
        P("step", "gz", None),
        P("gz", None),
    )
    return jax.shard_map(
        shards, mesh=mesh, in_specs=placed, out_specs=P("step", "gz", None, None), check_vma=False
    )
```

```python
import math

import jax
import jax.numpy as jnp
from jax import lax
from jax.experimental import pallas as pl
from jax.experimental.pallas import tpu as pltpu
from jax.sharding import PartitionSpec as P

SB = 16
HALO = 3
PAD = 8
MIB = 1024 * 1024


def offsets(code):
    return (
        lax.div(code, 25) - 2,
        lax.rem(lax.div(code, 5), 5) - 2,
        lax.rem(code, 5) - 2,
    )


def fit_kernel(
    settings_hbm, r_ref, d_ref, inner_ref, outer_ref,
    own_out, edge_out, deep, left, right, settings, arrived
):
    planes, channels, rows, width = r_ref.shape
    depth = channels * SB
    window = planes + 2
    fetch = pltpu.make_async_copy(settings_hbm, settings, arrived)
    fetch.start()
    lane = lax.broadcasted_iota(jnp.int32, (1, width), 1)
    line = lax.broadcasted_iota(jnp.int32, (width, width), 0)
    column = lax.broadcasted_iota(jnp.int32, (width, width), 1)
    scale = 1.0 / math.sqrt(planes * depth * width)
    bend_row = jnp.ones((1, width), jnp.float32)
    slope_row = jnp.zeros((1, width), jnp.float32)
    centre_row = jnp.zeros((1, width), jnp.float32)
    quality_row = jnp.ones((1, width), jnp.float32)
    tether_row = jnp.ones((1, width), jnp.float32)
    zeros = jnp.zeros((channels, PAD, width), jnp.float32)
    fetch.wait()
    parity = lax.rem(lax.axis_index("gz"), 2)
    inner_at = (1 - parity) * (planes + HALO)
    outer_at = parity * (planes + HALO)
    for z in range(planes + 2 * HALO):
        deep[z, :, 0:PAD, :] = zeros
        deep[z, :, PAD + rows : 2 * PAD + rows, :] = zeros
    for z in range(HALO):
        deep[inner_at + z, :, PAD : PAD + rows, :] = inner_ref[z].astype(jnp.float32)
        deep[outer_at + z, :, PAD : PAD + rows, :] = outer_ref[z].astype(jnp.float32)
    for z in range(planes):
        deep[z + HALO, :, PAD : PAD + rows, :] = d_ref[z].astype(jnp.float32)

    for block in range(rows // SB):
        shifts = offsets(settings[0, block].astype(jnp.int32))
        for z in range(planes):
            plane = r_ref[z, :, block * SB : (block + 1) * SB, :].astype(jnp.float32)
            turned = plane.reshape(depth, width).T.astype(jnp.bfloat16)
            left[:, z * depth : (z + 1) * depth] = turned
        first_plane = shifts[0] + (HALO - 1)
        first_row = shifts[1] + (PAD - 1 + block * SB)
        for p in range(window):
            for ty in range(3):
                part = deep[first_plane + p, :, pl.ds(first_row + ty, SB), :]
                right[p * depth : (p + 1) * depth, ty * width : (ty + 1) * width] = (
                    part.reshape(depth, width).astype(jnp.bfloat16)
                )
        grams = [
            jnp.dot(
                left[...],
                right[tz * depth : (tz + planes) * depth, :],
                preferred_element_type=jnp.float32,
            )
            for tz in range(3)
        ]
        cut = [[gram[:, ty * width : (ty + 1) * width] for ty in range(3)] for gram in grams]
        along_z = [cut[t][0] + cut[t][1] + cut[t][2] for t in range(3)]
        along_y = [cut[0][t] + cut[1][t] + cut[2][t] for t in range(3)]
        whole = along_z[0] + along_z[1] + along_z[2]
        far = column - line - shifts[2]
        band = jnp.abs(far) <= 1
        upper = jnp.where(far == 1, whole, 0.0)
        lower = jnp.where(far == -1, whole, 0.0)
        middle = jnp.where(far == 0, whole, 0.0)
        bends = [
            jnp.where(band, 2.0 * g[1] - g[0] - g[2], 0.0) for g in (along_z, along_y)
        ] + [2.0 * middle - lower - upper]
        slopes = [jnp.where(band, g[2] - g[0], 0.0) for g in (along_z, along_y)] + [upper - lower]

        def total(values):
            return jnp.sum(jnp.sum(values, axis=0, keepdims=True), axis=1, keepdims=True) * scale

        sums = [jnp.maximum(total(b), 1.0) for b in bends]
        quality = (sums[0] + sums[1] + sums[2]) / 3.0
        for axis, shift in enumerate(shifts):
            here = lane == block * 3 + axis
            bend_row = jnp.where(here, sums[axis], bend_row)
            slope_row = jnp.where(here, total(slopes[axis]), slope_row)
            centre_row = jnp.where(here, shift.astype(jnp.float32), centre_row)
            quality_row = jnp.where(here, quality, quality_row)
            tether_row = jnp.where(here, settings[0, rows // SB + block], tether_row)

    measured = centre_row + jnp.clip(slope_row / (2.0 * bend_row), -1.0, 1.0)
    gain = quality_row / (quality_row + tether_row)
    other = jnp.where(lane < 3, pltpu.roll(measured, width - 3, 1), pltpu.roll(measured, 3, 1))
    used = lane < 6
    filtered = jnp.where(used, 2.0 * measured + other, 0.0)
    gain = jnp.where(used, gain, 0.0)
    own_out[...] = filtered + pltpu.roll(gain, 8, 1)
    edge_out[...] = pltpu.roll(filtered, 16, 1)


def track_kernel(all_ref, out_ref):
    step, slab, slabs = lax.axis_index("step"), lax.axis_index("gz"), lax.axis_size("gz")
    parity = lax.rem(slab, 2)
    steps = all_ref.shape[0] // 2
    width = all_ref.shape[2]
    lane = lax.broadcasted_iota(jnp.int32, (1, width), 1)
    weight_z = 2.0 + (slab > 0).astype(jnp.float32) + (slab < slabs - 1).astype(jnp.float32)
    weight = jnp.full((1, width), weight_z * 3.0, jnp.float32)
    state = jnp.zeros((1, width), jnp.float32)
    head = all_ref[0:steps, 0, :]
    tail = all_ref[steps : 2 * steps, 0, :]
    mine = jnp.where(parity == 0, head, tail)
    inner = jnp.where(parity == 0, tail, head)
    outer = pltpu.roll(mine, width - 16, 1)
    gain = pltpu.roll(mine, width - 8, 1)
    smooth = (outer + 2.0 * mine + inner) / weight
    keep = 1.0 - gain
    drive = gain * smooth
    for s in range(steps):
        new = keep[s : s + 1] * state + drive[s : s + 1]
        state = jnp.where(s <= step, new, state)
    state = jnp.where(lane < 6, state, 0.0)
    out_ref[0, 0, 0:1, :] = state[:, 0:3]
    out_ref[0, 0, 1:2, :] = pltpu.roll(state, width - 3, 1)[:, 0:3]


def shards(reference_volume, deformed, centres, tether):
    steps, slabs = lax.axis_size("step"), lax.axis_size("gz")
    slab, step = lax.axis_index("gz"), lax.axis_index("step")
    parity = slab & 1
    volume_now = deformed[0]
    planes, channels, rows, width = volume_now.shape
    depth = channels * SB
    window = planes + 2
    blocks = rows // SB
    vmem = pl.BlockSpec(memory_space=pltpu.VMEM)
    anywhere = pl.BlockSpec(memory_space=pl.ANY)
    like = jax.ShapeDtypeStruct

    inside = [(i, i ^ 1) for i in range(slabs)]
    outside = [(i, i + 1) for i in range(1, slabs - 1, 2)]
    outside = outside + [(j, i) for i, j in outside]
    far = planes - HALO
    to_inner = lax.dynamic_slice_in_dim(volume_now, (1 - parity) * far, HALO, 0)
    to_outer = lax.dynamic_slice_in_dim(volume_now, parity * far, HALO, 0)
    copies = jnp.broadcast_to(reference_volume[None], (steps,) + reference_volume.shape)
    outer = lax.ppermute(to_outer, "gz", outside)
    inner = lax.ppermute(to_inner, "gz", inside)
    gathered = lax.all_to_all(copies, "step", split_axis=0, concat_axis=0, tiled=True)
    whole_ref = gathered.transpose(1, 2, 0, 3, 4).reshape(planes, channels, rows, width)

    settings = jnp.concatenate([centres[0, 0].astype(jnp.float32), tether[0]])[None]
    own, edge = pl.pallas_call(
        fit_kernel,
        out_shape=[like((1, width), jnp.float32)] * 2,
        in_specs=[anywhere] + [vmem] * 4,
        out_specs=[vmem] * 2,
        scratch_shapes=[
            pltpu.VMEM((planes + 2 * HALO, channels, rows + 2 * PAD, width), jnp.float32),
            pltpu.VMEM((width, planes * depth), jnp.bfloat16),
            pltpu.VMEM((window * depth, 3 * width), jnp.bfloat16),
            pltpu.SMEM((1, 2 * blocks), jnp.float32),
            pltpu.SemaphoreType.DMA,
        ],
        compiler_params=pltpu.CompilerParams(vmem_limit_bytes=40 * MIB),
        name="fit",
    )(settings, whole_ref, volume_now, inner, outer)

    edge = lax.ppermute(edge, "gz", outside)
    row = (own + edge)[None]
    group = 2 * steps
    groups = [[group * i + j for j in range(group)] for i in range(slabs // 2)]
    everyone = lax.all_to_all(
        jnp.broadcast_to(row, (group, 1, width)),
        ("gz", "step"), split_axis=0, concat_axis=0, tiled=True, axis_index_groups=groups,
    )
    return pl.pallas_call(
        track_kernel,
        out_shape=like((1, 1, blocks, 3), jnp.float32),
        in_specs=[vmem],
        out_specs=vmem,
        compiler_params=pltpu.CompilerParams(vmem_limit_bytes=2 * MIB),
        name="track",
    )(everyone)


def solution(mesh):
    placed = (
        P("gz", None, "step", None),
        P("step", "gz", None, None, None),
        P("step", "gz", None),
        P("gz", None),
    )
    return jax.shard_map(
        shards, mesh=mesh, in_specs=placed, out_specs=P("step", "gz", None, None), check_vma=False
    )
```
